32 devices in a mesh: pitch: 4 (over y, x), span: 8 (over z, core).
Axes of the slice: x: 2, y: 2, z: 4, core: 2. Of those that a mesh axis runs over, the one named last changes fastest.
Arguments:
- flow_state: float32 [4, 128, 512, 128], P(None, 'span', 'pitch'), may hold values from -0.36 to 3.4, as said below
- node_offset: float32 [2, 128, 512, 128], P(None, 'span', 'pitch'), may hold values from -0.1 to 0.1
- blade_mode: float32 [2, 128, 128], P(None, 'span'), may hold values from -0.2 to 0.2
- phase_angles: float32 [2], replicated, may hold values from -3.140625 to 3.140625
- lag_series: float32 [2, 3, 2, 4, 128, 128], P(None, None, None, None, 'span'), may hold values from -0.3 to 0.3, as said below
Outputs:
- new_state: float32 [4, 128, 512, 128], P(None, 'span', 'pitch')
- moved_offset: float32 [2, 128, 512, 128], P(None, 'span', 'pitch')
The draws below stay inside these ranges and needn't reach their ends.
Inputs may be any that keep to these rules, and one draw needn't show every extreme that they name: `flow_state`: built from density in 0.8 to 1.2, velocity components within 0.3 and pressure in 0.7 to 1.3. `lag_series`: entries for density lie within 0.01.
All inputs are finite; a program needn't handle non-finite values.
Results may differ from the reference program's by a relative error of at most 0.00002.
Values sent between devices are 32-bit elements; how exact they have to be, the bound alone decides.
A program may use at most 192 MiB of HBM per device.

```python
import jax
import jax.numpy as jnp
from jax import lax

R = 128
HARM = 3
NA = 128
NP = 512


def draw_flow_state(key, part):
    key_list = jax.random.split(key, 4)
    grid_shape = (NA, NP, R)
    first_draw = jax.random.uniform(key_list[0], grid_shape, jnp.float32, -1.0, 1.0)
    second_draw = jax.random.uniform(key_list[1], grid_shape, jnp.float32, -1.0, 1.0)
    third_draw = jax.random.uniform(key_list[2], grid_shape, jnp.float32, -1.0, 1.0)
    fourth_draw = jax.random.uniform(key_list[3], grid_shape, jnp.float32, -1.0, 1.0)
    density = 1.0 + 0.2 * first_draw
    vel_x = 0.3 * second_draw
    vel_y = 0.3 * third_draw
    pressure = 1.0 + 0.3 * fourth_draw
    energy = pressure / 0.4 + 0.5 * density * (vel_x * vel_x + vel_y * vel_y)
    return jnp.stack([density, density * vel_x, density * vel_y, energy])


def draw_lag_series(key, part):
    values = jax.random.uniform(key, (2, HARM, 2, 4, NA, R), jnp.float32, -1.0, 1.0)
    var_scale = jnp.array([0.01, 0.3, 0.3, 0.3], jnp.float32)
    return values * var_scale[None, None, None, :, None, None]


def level_of(key, extent, cuts, low, top_value):
    def one(position, parts):
        heights = jax.random.uniform(jax.random.fold_in(jax.random.fold_in(key, 6), position), (parts,), jnp.float32, low / len(cuts), top_value / len(cuts))
        return jnp.repeat(jnp.exp(heights), extent[position] // parts).reshape((-1,) + (1,) * (len(extent) - position - 1))

    gain = one(*cuts[0])
    for cut in cuts[1:]:
        gain = gain * one(*cut)
    return gain


def setup_inputs(seed: int = 0) -> dict:
    key_of = jax.random.split(jax.random.key(seed), 6)
    return {
        "flow_state": draw_flow_state(jax.random.fold_in(key_of[5], 71), 0),
        "node_offset": jnp.clip(jax.random.uniform(key_of[1], (2, NA, NP, R), jnp.float32, -0.1, 0.1) * level_of(key_of[1], (2, NA, NP, R), ((1, 8), (2, 4)), -0.4, 0.0), -0.1, 0.1),
        "blade_mode": jnp.clip(jax.random.uniform(key_of[2], (2, NA, R), jnp.float32, -0.2, 0.2) * level_of(key_of[2], (2, NA, R), ((1, 8),), -0.4, 0.0), -0.2, 0.2),
        "phase_angles": jnp.clip(jax.random.uniform(key_of[3], (2,), jnp.float32, -3.140625, 3.140625), -3.140625, 3.140625),
        "lag_series": draw_lag_series(jax.random.fold_in(key_of[5], 71), 0),
    }


HEAT_RATIO = 1.4
TIME_STEP = 0.25
DAMPING = 0.02
SECTION_WEIGHTS = (0.5, 1.0)

def extend_linear(values, axis_pos):
    length = values.shape[axis_pos]
    first_row = lax.slice_in_dim(values, 0, 1, axis=axis_pos)
    second_row = lax.slice_in_dim(values, 1, 2, axis=axis_pos)
    last_row = lax.slice_in_dim(values, length - 1, length, axis=axis_pos)
    before_row = lax.slice_in_dim(values, length - 2, length - 1, axis=axis_pos)
    step_low = first_row - second_row
    step_high = last_row - before_row
    return jnp.concatenate([first_row + 2.0 * step_low, first_row + step_low, values, last_row + step_high, last_row + 2.0 * step_high], axis=axis_pos)

def radial_damping(values, axis_pos):
    count = values.shape[axis_pos]
    first_row = lax.slice_in_dim(values, 0, 1, axis=axis_pos)
    last_row = lax.slice_in_dim(values, count - 1, count, axis=axis_pos)
    extended = jnp.concatenate([first_row, first_row, values, last_row, last_row], axis=axis_pos)
    return lax.slice_in_dim(extended, 4, 4 + count, axis=axis_pos) - 4.0 * lax.slice_in_dim(extended, 3, 3 + count, axis=axis_pos) + 6.0 * values - 4.0 * lax.slice_in_dim(extended, 1, 1 + count, axis=axis_pos) + lax.slice_in_dim(extended, 0, count, axis=axis_pos)

def unit_normal(earlier, later):
    along_x = later[0] - earlier[0]
    along_y = 1.0 + later[1] - earlier[1]
    length = jnp.sqrt(along_x * along_x + along_y * along_y)
    return jnp.stack([along_x / length, along_y / length])

def wall_amplitude(shape_mode, angle, blade_mask):
    return (shape_mode[0] * jnp.cos(angle) - shape_mode[1] * jnp.sin(angle)) * blade_mask

def lag_shift(series, phase_now, phase_move):
    series_sum = jnp.zeros(series.shape[2:], jnp.float32)
    for number in range(series.shape[0]):
        harmonic = float(number + 1)
        change_cos = jnp.cos(harmonic * (phase_now + phase_move)) - jnp.cos(harmonic * phase_now)
        change_sin = jnp.sin(harmonic * (phase_now + phase_move)) - jnp.sin(harmonic * phase_now)
        series_sum = series_sum + series[number, 0] * change_cos - series[number, 1] * change_sin
    return series_sum

def metric_terms(offset_x, offset_y):
    x_zeta = 1.0 + (offset_x[..., 2:, 1:-1] - offset_x[..., :-2, 1:-1]) * 0.5
    x_xi = (offset_x[..., 1:-1, 2:] - offset_x[..., 1:-1, :-2]) * 0.5
    y_xi = 1.0 + (offset_y[..., 1:-1, 2:] - offset_y[..., 1:-1, :-2]) * 0.5
    y_zeta = (offset_y[..., 2:, 1:-1] - offset_y[..., :-2, 1:-1]) * 0.5
    return (x_zeta, x_xi, y_xi, y_zeta)

def geometry(grid_pad):
    x_zeta, x_xi, y_xi, y_zeta = metric_terms(grid_pad[0], grid_pad[1])
    old_zeta, old_xi, oldy_xi, oldy_zeta = metric_terms(grid_pad[0] - grid_pad[2], grid_pad[1] - grid_pad[3])
    volume_new = (x_zeta * y_xi - x_xi * y_zeta)[..., 1:-1, 1:-1]
    volume_old = (old_zeta * oldy_xi - old_xi * oldy_zeta)[..., 1:-1, 1:-1]
    speed_x = grid_pad[2][..., 1:-1, 1:-1] / TIME_STEP
    speed_y = grid_pad[3][..., 1:-1, 1:-1] / TIME_STEP
    first_pitch = -y_zeta
    second_pitch = x_zeta
    sweep_pitch = first_pitch * speed_x + second_pitch * speed_y
    first_axial = y_xi
    second_axial = -x_xi
    sweep_axial = first_axial * speed_x + second_axial * speed_y
    return ((first_pitch, second_pitch, sweep_pitch, first_axial, second_axial, sweep_axial), volume_old, volume_new)

def directional(strip_cells, first_coef, second_coef, sweep_term):
    density = strip_cells[0]
    vel_x = strip_cells[1] / density
    vel_y = strip_cells[2] / density
    energy = strip_cells[3]
    pressure = (HEAT_RATIO - 1.0) * (energy - 0.5 * density * (vel_x * vel_x + vel_y * vel_y))
    flux_x = jnp.stack([strip_cells[1], strip_cells[1] * vel_x + pressure, strip_cells[1] * vel_y, (energy + pressure) * vel_x])
    flux_y = jnp.stack([strip_cells[2], strip_cells[2] * vel_x, strip_cells[2] * vel_y + pressure, (energy + pressure) * vel_y])
    return first_coef * flux_x + second_coef * flux_y - sweep_term * strip_cells

def planar_residual(padded, geo_terms):
    first_pitch, second_pitch, sweep_pitch, first_axial, second_axial, sweep_axial = geo_terms
    pitch_flux = directional(padded[..., 2:-2, 1:-1], first_pitch[..., 1:-1, :], second_pitch[..., 1:-1, :], sweep_pitch[..., 1:-1, :])
    axial_flux = directional(padded[..., 1:-1, 2:-2], first_axial[..., :, 1:-1], second_axial[..., :, 1:-1], sweep_axial[..., :, 1:-1])
    divergence = (pitch_flux[..., 2:] - pitch_flux[..., :-2]) * 0.5 + (axial_flux[..., 2:, :] - axial_flux[..., :-2, :]) * 0.5
    centre = padded[..., 2:-2, 2:-2]
    fourth = padded[..., 2:-2, 4:] - 4.0 * padded[..., 2:-2, 3:-1] + 6.0 * centre - 4.0 * padded[..., 2:-2, 1:-3] + padded[..., 2:-2, :-4] + (padded[..., 4:, 2:-2] - 4.0 * padded[..., 3:-1, 2:-2] + 6.0 * centre - 4.0 * padded[..., 1:-3, 2:-2] + padded[..., :-4, 2:-2])
    return divergence + DAMPING * fourth

def flow_ghosts(row_zero, row_one, row_last, row_before, wrap_low0, wrap_low1, wrap_high0, wrap_high1, blade_flag, corr_low, corr_high):
    sign_flip = jnp.array([1.0, 1.0, -1.0, 1.0], jnp.float32).reshape((4,) + (1,) * (row_zero.ndim - 1))
    ghost_m2 = jnp.where(blade_flag, row_one * sign_flip, wrap_low0 + corr_low)
    ghost_m1 = jnp.where(blade_flag, row_zero * sign_flip, wrap_low1 + corr_low)
    ghost_p0 = jnp.where(blade_flag, row_last * sign_flip, wrap_high0 + corr_high)
    ghost_p1 = jnp.where(blade_flag, row_before * sign_flip, wrap_high1 + corr_high)
    return (ghost_m2, ghost_m1, ghost_p0, ghost_p1)

def reference(flow_state, node_offset, blade_mode, phase_angles, lag_series):
    axial_index = jnp.arange(NA, dtype=jnp.int32)
    lead_edge = NA // 4
    blade_flag = (axial_index >= lead_edge) & (axial_index < NA - lead_edge)
    blade_mask = blade_flag.astype(jnp.float32)
    blend_row = jnp.arange(NP, dtype=jnp.int32).astype(jnp.float32) / (NP - 1)
    phase_now = phase_angles[0]
    phase_lag = phase_angles[1]

    def surface_geometry(pieces):
        offsets, shape_mode = pieces
        low_wall = wall_amplitude(shape_mode, phase_now, blade_mask) * unit_normal(offsets[..., 0], offsets[..., 1])
        high_wall = wall_amplitude(shape_mode, phase_now + phase_lag, blade_mask) * unit_normal(offsets[..., NP - 2], offsets[..., NP - 1])
        shift_field = (1.0 - blend_row) * low_wall[..., None] + blend_row * high_wall[..., None]
        moved = offsets + shift_field
        grid_field = jnp.concatenate([moved, shift_field], 0)
        grid_pad = extend_linear(extend_linear(grid_field, 1), 2)
        geo_terms, volume_old, volume_new = geometry(grid_pad)
        return (moved, geo_terms, volume_old, volume_new)
    moved_r, geo_r, old_r, new_r = lax.map(surface_geometry, (jnp.moveaxis(node_offset, -1, 0), jnp.moveaxis(blade_mode, -1, 0)))
    corr_low_r = jnp.moveaxis(lag_shift(lag_series[1], phase_now, -phase_lag), -1, 0)
    corr_high_r = jnp.moveaxis(lag_shift(lag_series[0], phase_now, phase_lag), -1, 0)

    def surface_residual(pieces):
        current, geo_terms, corr_low, corr_high = pieces
        ghost_m2, ghost_m1, ghost_p0, ghost_p1 = flow_ghosts(current[..., 0], current[..., 1], current[..., NP - 1], current[..., NP - 2], current[..., NP - 2], current[..., NP - 1], current[..., 0], current[..., 1], blade_flag, corr_low, corr_high)
        padded = jnp.concatenate([ghost_m2[..., None], ghost_m1[..., None], current, ghost_p0[..., None], ghost_p1[..., None]], -1)
        padded = jnp.concatenate([padded[..., 0:1, :], padded[..., 0:1, :], padded, padded[..., -1:, :], padded[..., -1:, :]], -2)
        return planar_residual(padded, geo_terms)
    start_r = jnp.moveaxis(flow_state, -1, 0)
    current_r = start_r
    for weight in SECTION_WEIGHTS:
        planar = lax.map(surface_residual, (current_r, geo_r, corr_low_r, corr_high_r))
        total = planar + DAMPING * radial_damping(current_r, 0)
        current_r = (old_r[:, None] * start_r - weight * TIME_STEP * total) / new_r[:, None]
    return (jnp.moveaxis(current_r, 0, -1), jnp.moveaxis(moved_r, 0, -1))
```

```python
import functools

import jax
import jax.numpy as jnp
from jax import lax
from jax.experimental import pallas as pl
from jax.experimental.pallas import tpu as pltpu
from jax.sharding import PartitionSpec as P

MESH = pl.DeviceIdType.MESH
F32 = jnp.float32
TIME_STEP = 0.25
DAMPING = 0.02
SECTION_WEIGHTS = (0.5, 1.0)
PAD = 8
CHUNK = 16


def kernel(
    n_pitch, n_span, AL, PL, R, HARM,
    phase, flow_hbm, node_hbm, mode, lag,
    state_out, moved_out,
    S0, S1, N, M, GE, H, G, RAD, W, MODE, CORR, TRIG, SB0, RB0, SB1, RB1, CS, CR,
    loc, send, recv, wsend, wrecv, osem,
):
    me_p = lax.axis_index("pitch")
    me_s = lax.axis_index("span")
    left = lax.rem(me_p + n_pitch - 1, n_pitch)
    right = lax.rem(me_p + 1, n_pitch)
    low_end = me_p == 0
    high_end = me_p == n_pitch - 1
    first = me_s == 0
    last = me_s == n_span - 1
    not_first = me_s > 0
    not_last = me_s < n_span - 1
    total_pitch = PL * n_pitch
    total_axial = AL * n_span
    lead = total_axial // 4
    lo, hi = PAD, PAD + PL
    def by_rows(count, body, step):
        def several(i, _):
            for j in range(step):
                body(i * step + j, 0)
            return 0

        lax.fori_loop(0, count // step, several, 0)

    def remote(src, dst, number, p, s):
        return pltpu.make_async_remote_copy(
            src_ref=src, dst_ref=dst, send_sem=send.at[number], recv_sem=recv.at[number],
            device_id=(p, s), device_id_type=MESH,
        )

    node_in = pltpu.make_async_copy(
        node_hbm, N.at[:, pl.ds(1, AL), pl.ds(lo, PL), :], loc.at[0]
    )
    flow_in = pltpu.make_async_copy(
        flow_hbm, S0.at[:, pl.ds(2, AL), pl.ds(lo, PL), :], loc.at[1]
    )
    node_in.start()
    flow_in.start()

    above = lax.rem(me_s + n_span - 1, n_span)
    below = lax.rem(me_s + 1, n_span)

    barrier = pltpu.get_barrier_semaphore()
    for step in range(1, n_pitch):
        other = lax.rem(me_p + step, n_pitch)
        pl.semaphore_signal(barrier, inc=1, device_id=(other, me_s), device_id_type=MESH)

    @pl.when(not_first)
    def _():
        for other in range(n_pitch):
            pl.semaphore_signal(
                barrier, inc=1, device_id=(other, above), device_id_type=MESH
            )

    @pl.when(not_last)
    def _():
        for other in range(n_pitch):
            pl.semaphore_signal(
                barrier, inc=1, device_id=(other, below), device_id_type=MESH
            )

    rows = lax.broadcasted_iota(jnp.int32, (16, R), 0)
    harmonic = jnp.where(rows < 2, 0, lax.rem(rows + 1, 3)) + 1
    move = jnp.where(rows == 1, 1, jnp.where(rows < 2, 0, jnp.where(rows < 5, -1, jnp.where(rows < 8, 0, 1))))
    now = phase[0]
    lagging = phase[1]
    angle = harmonic.astype(F32) * (now + move.astype(F32) * lagging)
    TRIG[0] = jnp.cos(angle)
    TRIG[1] = jnp.sin(angle)

    def trig(kind, row):
        return TRIG[kind, row:row + 1, :]

    for side, base in ((0, 2), (1, 8)):
        series = 1 - side
        for var in range(4):
            total = None
            for k in range(HARM):
                change_cos = trig(0, base + k) - trig(0, 5 + k)
                change_sin = trig(1, base + k) - trig(1, 5 + k)
                term = lag[series, k, 0, var] * change_cos - lag[series, k, 1, var] * change_sin
                total = term if total is None else total + term
            for a in range(AL):
                CORR[side, var, a] = total[a:a + 1, :]
    for part in range(2):
        for a in range(AL):
            MODE[part, a] = mode[part, a:a + 1, :]

    def blade_at(a):
        at = me_s * AL + a
        return (at >= lead) & (at < total_axial - lead)

    node_in.wait()

    def wall_rows(side, early, late):
        def body(a, _):
            nx = N[0, a + 1, late:late + 1, :] - N[0, a + 1, early:early + 1, :]
            ny = 1.0 + N[1, a + 1, late:late + 1, :] - N[1, a + 1, early:early + 1, :]
            length = jnp.sqrt(nx * nx + ny * ny)
            amp = MODE[0, a] * trig(0, side) - MODE[1, a] * trig(1, side)
            amp = jnp.where(blade_at(a), amp, 0.0)
            W[side, 0, a + 1] = amp * (nx / length)
            W[side, 1, a + 1] = amp * (ny / length)
            return 0

        by_rows(AL, body, 8)

    @pl.when(low_end)
    def _():
        wall_rows(0, lo, lo + 1)

    @pl.when(high_end)
    def _():
        wall_rows(1, hi - 2, hi - 1)

    for left_row, src in ((0, hi - 1), (1, lo)):
        for end, a in ((0, AL), (1, 1)):
            number = 2 * end + left_row
            CS[number] = N[:, a, src:src + 1, :]

    sides = jnp.where(not_first, 1, 0) + jnp.where(not_last, 1, 0)
    pl.semaphore_wait(barrier, n_pitch - 1 + n_pitch * sides)

    def wall_copy(side, kind, p, s, step):
        src, dst = ((1, 1), (1, AL + 1), (AL, 0))[kind]
        size = AL if kind == 0 else 1
        return pltpu.make_async_remote_copy(
            src_ref=W.at[side, :, pl.ds(src, size)],
            dst_ref=W.at[side, :, pl.ds(dst, size)],
            send_sem=wsend.at[(side * 3 + kind) * n_pitch + step],
            recv_sem=wrecv.at[side * 3 + kind],
            device_id=(p, s), device_id_type=MESH,
        )

    def walls(act):
        for side, own in ((0, low_end), (1, high_end)):
            @pl.when(own)
            def _(side=side):
                for step in range(1, n_pitch):
                    act(wall_copy(side, 0, lax.rem(me_p + step, n_pitch), me_s, step))

                @pl.when(not_first)
                def _():
                    for other in range(n_pitch):
                        act(wall_copy(side, 1, other, above, other))

                @pl.when(not_last)
                def _():
                    for other in range(n_pitch):
                        act(wall_copy(side, 2, other, below, other))

    walls(lambda copy: copy.start())

    field = pl.ds(lo, PL)
    node_up = remote(node_hbm.at[:, pl.ds(0, 1)], N.at[:, pl.ds(AL + 1, 1), field], 0, me_p, above)
    node_down = remote(node_hbm.at[:, pl.ds(AL - 1, 1)], N.at[:, pl.ds(0, 1), field], 1, me_p, below)
    flow_up = remote(flow_hbm.at[:, pl.ds(0, 2)], S0.at[:, pl.ds(AL + 2, 2), field], 2, me_p, above)
    flow_down = remote(flow_hbm.at[:, pl.ds(AL - 2, 2)], S0.at[:, pl.ds(0, 2), field], 3, me_p, below)
    to_left = remote(SB0.at[0], RB0.at[1], 4, left, me_s)
    to_right = remote(SB0.at[1], RB0.at[0], 5, right, me_s)
    corner_down = [
        remote(CS.at[0], CR.at[0], 6, right, below),
        remote(CS.at[1], CR.at[1], 7, left, below),
    ]
    corner_up = [
        remote(CS.at[2], CR.at[2], 8, right, above),
        remote(CS.at[3], CR.at[3], 9, left, above),
    ]
    next_up = remote(S1.at[:, pl.ds(2, 2), field], S1.at[:, pl.ds(AL + 2, 2), field], 10, me_p, above)
    next_down = remote(S1.at[:, pl.ds(AL, 2), field], S1.at[:, pl.ds(0, 2), field], 11, me_p, below)
    next_left = remote(SB1.at[0], RB1.at[1], 12, left, me_s)
    next_right = remote(SB1.at[1], RB1.at[0], 13, right, me_s)

    @pl.when(not_first)
    def _():
        node_up.start()
        for copy in corner_up:
            copy.start()
        flow_up.start()

    @pl.when(not_last)
    def _():
        node_down.start()
        for copy in corner_down:
            copy.start()
        flow_down.start()

    flow_in.wait()

    def pack(S, B):
        def body(a, _):
            for var in range(4):
                B[0, var, a] = S[var, a + 2, lo:lo + 2, :]
                B[1, var, a] = S[var, a + 2, hi - 2:hi, :]
            return 0

        by_rows(AL, body, 4)

    def pack_node(a, _):
        for var in range(2):
            SB0[0, 4 + var, a] = N[var, a + 1, lo:lo + 2, :]
            SB0[1, 4 + var, a] = N[var, a + 1, hi - 2:hi, :]
        return 0

    pack(S0, SB0)
    by_rows(AL, pack_node, 4)
    to_left.start()
    to_right.start()

    to_left.wait_recv()
    to_right.wait_recv()

    def node_edges(a, _):
        for var in range(2):
            N[var, a + 1, lo - 1:lo, :] = RB0[0, 4 + var, a, 1:2, :]
            N[var, a + 1, hi:hi + 1, :] = RB0[1, 4 + var, a, 0:1, :]
        return 0

    by_rows(AL, node_edges, 4)

    @pl.when(not_first)
    def _():
        node_down.wait_recv()
        for copy in corner_down:
            copy.wait_recv()
        N[:, 0, lo - 1:lo, :] = CR[0]
        N[:, 0, hi:hi + 1, :] = CR[1]

    @pl.when(not_last)
    def _():
        node_up.wait_recv()
        for copy in corner_up:
            copy.wait_recv()
        N[:, AL + 1, lo - 1:lo, :] = CR[2]
        N[:, AL + 1, hi:hi + 1, :] = CR[3]

    @pl.when(first)
    def _():
        for var in range(2):
            N[var, 0] = 2.0 * N[var, 1] - N[var, 2]

    @pl.when(last)
    def _():
        for var in range(2):
            N[var, AL + 1] = 2.0 * N[var, AL] - N[var, AL - 1]

    @pl.when(low_end)
    def _():
        def body(a, _):
            for var in range(2):
                N[var, a, lo - 1:lo, :] = 2.0 * N[var, a, lo:lo + 1, :] - N[var, a, lo + 1:lo + 2, :]
            return 0

        lax.fori_loop(0, AL + 2, body, 0)

    @pl.when(high_end)
    def _():
        def body(a, _):
            for var in range(2):
                N[var, a, hi:hi + 1, :] = 2.0 * N[var, a, hi - 1:hi, :] - N[var, a, hi - 2:hi - 1, :]
            return 0

        lax.fori_loop(0, AL + 2, body, 0)

    low_gate = jnp.where(low_end, 1.0, 0.0)
    high_gate = jnp.where(high_end, 1.0, 0.0)

    def pitch_edges(S, B):
        def body(a, _):
            blade = blade_at(a)
            low_wall = blade & low_end
            high_wall = blade & high_end
            for var in range(4):
                sign = -1.0 if var == 2 else 1.0
                low_corr = CORR[0, var, a] * low_gate
                high_corr = CORR[1, var, a] * high_gate
                for row in range(2):
                    mirror = S[var, a + 2, lo + 1 - row:lo + 2 - row, :] * sign
                    arrived = B[0, var, a, row:row + 1, :] + low_corr
                    S[var, a + 2, lo - 2 + row:lo - 1 + row, :] = jnp.where(low_wall, mirror, arrived)
                    mirror = S[var, a + 2, hi - 1 - row:hi - row, :] * sign
                    arrived = B[1, var, a, row:row + 1, :] + high_corr
                    S[var, a + 2, hi + row:hi + row + 1, :] = jnp.where(high_wall, mirror, arrived)
            return 0

        by_rows(AL, body, 4)

    inner = [(q, CHUNK) for q in range(lo, hi, CHUNK)]
    outer = [(0, PAD), (hi, PAD)]

    def along_pitch(T, a, q, size):
        return [
            T[comp, a, q + 1:q + 1 + size, :] - T[comp, a, q - 1:q - 1 + size, :] for comp in range(2)
        ]

    def along_axis(T, a, q, size):
        return [T[comp, a + 1, q:q + size, :] - T[comp, a - 1, q:q + size, :] for comp in range(2)]

    def old_row(i, _):
        a = i + 1
        for q, size in inner:
            px, py = along_pitch(N, a, q, size)
            zx, zy = along_axis(N, a, q, size)
            GE[6, a, q:q + size, :] = (2.0 + zx) * (2.0 + py) - px * zy
        return 0

    pitch_edges(S0, RB0)
    lax.fori_loop(0, AL, old_row, 0)

    for side, own in ((0, low_end), (1, high_end)):
        @pl.when(jnp.logical_not(own))
        def _(side=side):
            wall_copy(side, 0, me_p, me_s, 0).wait_recv()

        @pl.when(not_last)
        def _(side=side):
            wall_copy(side, 1, me_p, me_s, 0).wait_recv()

        @pl.when(not_first)
        def _(side=side):
            wall_copy(side, 2, me_p, me_s, 0).wait_recv()

        @pl.when(first)
        def _(side=side):
            W[side, :, 0] = 2.0 * W[side, :, 1] - W[side, :, 2]

        @pl.when(last)
        def _(side=side):
            W[side, :, AL + 1] = 2.0 * W[side, :, AL] - W[side, :, AL - 1]

    def shift_of(a, q, size):
        at = me_p * PL + (q - lo) + lax.broadcasted_iota(jnp.int32, (size, R), 0)
        blend = at.astype(F32) * (1.0 / (total_pitch - 1))
        out = []
        for comp in range(2):
            low = W[0, comp, a]
            out.append(low + blend * (W[1, comp, a] - low))
        return out

    def move_row(a, _):
        for q, size in outer + inner:
            for comp, shift in enumerate(shift_of(a, q, size)):
                M[comp, a, q:q + size, :] = N[comp, a, q:q + size, :] + shift
        return 0

    lax.fori_loop(0, AL + 2, move_row, 0)
    moved_copy = pltpu.make_async_copy(M.at[:, pl.ds(1, AL), field], moved_out, osem.at[0])
    moved_copy.start()

    def axial_terms(a, q, size):
        px, py = along_pitch(M, a, q, size)
        c, e = 2.0 + py, -px
        sx, sy = shift_of(a, q, size)
        GE[3, a, q:q + size, :] = c
        GE[4, a, q:q + size, :] = e
        GE[5, a, q:q + size, :] = (c * sx + e * sy) * (1.0 / TIME_STEP)
        return c, e

    def pitch_terms(a, q, size):
        zx, zy = along_axis(M, a, q, size)
        first_c, second_c = -zy, 2.0 + zx
        sx, sy = shift_of(a, q, size)
        GE[0, a, q:q + size, :] = first_c
        GE[1, a, q:q + size, :] = second_c
        GE[2, a, q:q + size, :] = (first_c * sx + second_c * sy) * (1.0 / TIME_STEP)
        return first_c, second_c

    def metric_row(i, _):
        a = i + 1
        for q, size in outer:
            pitch_terms(a, q, size)
        for q, size in inner:
            c, e = axial_terms(a, q, size)
            first_c, second_c = pitch_terms(a, q, size)
            new = second_c * c - e * first_c
            inverse = 1.0 / new
            GE[6, a, q:q + size, :] = GE[6, a, q:q + size, :] * inverse
            GE[7, a, q:q + size, :] = TIME_STEP * inverse
        return 0

    for a in (0, AL + 1):
        for q, size in inner:
            axial_terms(a, q, size)
    lax.fori_loop(0, AL, metric_row, 0)

    def flux(S, a, q, size, pitch, axial):
        r, mx, my, e = [S[var, a + 1, q:q + size, :] for var in range(4)]
        guess = pl.reciprocal(r, approx=True)
        inverse = guess * (2.0 - r * guess)
        u = mx * inverse
        v = my * inverse
        p = 0.4 * e - 0.2 * (mx * u + my * v)
        done = []
        for wanted, base in ((pitch, 0), (axial, 3)):
            if not wanted:
                done.append(None)
                continue
            c0, c1, sweep = [GE[base + j, a, q:q + size, :] for j in range(3)]
            w = c0 * u + c1 * v
            rel = w - sweep
            done.append((r * rel, mx * rel + c0 * p, my * rel + c1 * p, e * rel + p * w))
        return done

    def flux_field(S):
        def body(i, _):
            a = i + 1
            for q, size in inner:
                pitch_flux, axial_flux = flux(S, a, q, size, True, True)
                for var in range(4):
                    G[var, i, q:q + size, :] = pitch_flux[var]
                    H[var, a, q - lo:q - lo + size, :] = axial_flux[var]
            return 0

        lax.fori_loop(0, AL, body, 0)

    def flux_sides(S):
        def body(i, _):
            for q, size in outer:
                pitch_flux, _unused = flux(S, i + 1, q, size, True, False)
                for var in range(4):
                    G[var, i, q:q + size, :] = pitch_flux[var]
            return 0

        lax.fori_loop(0, AL, body, 0)

    def flux_ends(S):
        for a in (0, AL + 1):
            for q, size in inner:
                _unused, axial_flux = flux(S, a, q, size, False, True)
                for var in range(4):
                    H[var, a, q - lo:q - lo + size, :] = axial_flux[var]

    at_row = lax.broadcasted_iota(jnp.int32, (R, R), 0)
    at_col = lax.broadcasted_iota(jnp.int32, (R, R), 1)
    radial = jnp.zeros((R, R), F32)
    for offset, weight in ((-2, 1.0), (-1, -4.0), (0, 6.0), (1, -4.0), (2, 1.0)):
        source = jnp.clip(at_col + offset, 0, R - 1)
        radial = radial + jnp.where(at_row == source, weight, 0.0)
    radial = jnp.concatenate([radial, radial], axis=0).astype(jnp.bfloat16)

    def residual_row(S, i, weight, put):
        a = i + 2
        for var in range(4):
            values = S[var, a, lo:hi, :]
            head = values.astype(jnp.bfloat16)
            tail = (values - head.astype(F32)).astype(jnp.bfloat16)
            RAD[var] = jnp.dot(
                jnp.concatenate([head, tail], axis=1), radial, preferred_element_type=F32
            )
        for q, size in inner:
            keep = GE[6, i + 1, q:q + size, :]
            rate = GE[7, i + 1, q:q + size, :] * weight
            h = q - lo
            for var in range(4):
                here = S[var, a, q:q + size, :]
                near = (S[var, a, q + 1:q + 1 + size, :] + S[var, a, q - 1:q - 1 + size, :]) + (
                    S[var, a + 1, q:q + size, :] + S[var, a - 1, q:q + size, :]
                )
                far = (S[var, a, q + 2:q + 2 + size, :] + S[var, a, q - 2:q - 2 + size, :]) + (
                    S[var, a + 2, q:q + size, :] + S[var, a - 2, q:q + size, :]
                )
                fourth = (far + RAD[var, h:h + size, :]) + (12.0 * here - 4.0 * near)
                change = (G[var, i, q + 1:q + 1 + size, :] - G[var, i, q - 1:q - 1 + size, :]) + (
                    H[var, i + 2, h:h + size, :] - H[var, i, h:h + size, :]
                )
                value = keep * S0[var, a, q:q + size, :] - rate * (change + (4.0 * DAMPING) * fourth)
                put(var, i, q, size, value)

    def put_one(var, i, q, size, value):
        S1[var, i + 2, q:q + size, :] = value

    def put_two(var, i, q, size, value):
        S0[var, i + 2, q:q + size, :] = value

    def residual_inner(S, weight, put):
        def body(i, _):
            residual_row(S, i + 2, weight, put)
            return 0

        lax.fori_loop(0, AL - 4, body, 0)

    def residual_ends(S, weight, put):
        def body(i, _):
            residual_row(S, i + (AL - 4) * (i // 2), weight, put)
            return 0

        lax.fori_loop(0, 4, body, 0)

    def axial_edges(S, down, up):
        @pl.when(not_first)
        def _():
            down.wait_recv()

        @pl.when(not_last)
        def _():
            up.wait_recv()

        @pl.when(first)
        def _():
            for var in range(4):
                row = S[var, 2, lo:hi, :]
                S[var, 0, lo:hi, :] = row
                S[var, 1, lo:hi, :] = row

        @pl.when(last)
        def _():
            for var in range(4):
                row = S[var, AL + 1, lo:hi, :]
                S[var, AL + 2, lo:hi, :] = row
                S[var, AL + 3, lo:hi, :] = row

    flux_field(S0)
    flux_sides(S0)
    residual_inner(S0, SECTION_WEIGHTS[0], put_one)
    axial_edges(S0, flow_down, flow_up)
    flux_ends(S0)
    residual_ends(S0, SECTION_WEIGHTS[0], put_one)

    @pl.when(not_first)
    def _():
        next_up.start()

    @pl.when(not_last)
    def _():
        next_down.start()

    pack(S1, SB1)
    next_left.start()
    next_right.start()

    flux_field(S1)
    next_left.wait_recv()
    next_right.wait_recv()
    pitch_edges(S1, RB1)
    flux_sides(S1)
    residual_inner(S1, SECTION_WEIGHTS[1], put_two)
    out_inner = pltpu.make_async_copy(
        S0.at[:, pl.ds(4, AL - 4), field], state_out.at[:, pl.ds(2, AL - 4)], osem.at[1]
    )
    out_inner.start()
    axial_edges(S1, next_down, next_up)
    flux_ends(S1)
    residual_ends(S1, SECTION_WEIGHTS[1], put_two)
    out_first = pltpu.make_async_copy(
        S0.at[:, pl.ds(2, 2), field], state_out.at[:, pl.ds(0, 2)], osem.at[2]
    )
    out_last = pltpu.make_async_copy(
        S0.at[:, pl.ds(AL, 2), field], state_out.at[:, pl.ds(AL - 2, 2)], osem.at[3]
    )
    out_first.start()
    out_last.start()

    walls(lambda copy: copy.wait_send())

    @pl.when(not_first)
    def _():
        for copy in [node_up, flow_up, next_up] + corner_up:
            copy.wait_send()

    @pl.when(not_last)
    def _():
        for copy in [node_down, flow_down, next_down] + corner_down:
            copy.wait_send()

    for copy in (to_left, to_right, next_left, next_right):
        copy.wait_send()
    moved_copy.wait()
    out_inner.wait()
    out_first.wait()
    out_last.wait()


def solution(mesh):
    n_pitch = mesh.shape["pitch"]
    n_span = mesh.shape["span"]

    def per_device(flow_state, node_offset, blade_mode, phase_angles, lag_series):
        _, AL, PL, R = flow_state.shape
        HARM = lag_series.shape[1]
        width = PL + 2 * PAD
        vmem = lambda *shape: pltpu.VMEM(shape, F32)
        dma = lambda count: pltpu.SemaphoreType.DMA((count,))
        return pl.pallas_call(
            functools.partial(kernel, n_pitch, n_span, AL, PL, R, HARM),
            out_shape=(
                jax.ShapeDtypeStruct(flow_state.shape, F32),
                jax.ShapeDtypeStruct(node_offset.shape, F32),
            ),
            in_specs=[
                pl.BlockSpec(memory_space=pltpu.SMEM),
                pl.BlockSpec(memory_space=pl.ANY),
                pl.BlockSpec(memory_space=pl.ANY),
                pl.BlockSpec(memory_space=pltpu.VMEM),
                pl.BlockSpec(memory_space=pltpu.VMEM),
            ],
            out_specs=(pl.BlockSpec(memory_space=pl.ANY), pl.BlockSpec(memory_space=pl.ANY)),
            scratch_shapes=[
                vmem(4, AL + 4, width, R),
                vmem(4, AL + 4, width, R),
                vmem(2, AL + 2, width, R),
                vmem(2, AL + 2, width, R),
                vmem(8, AL + 2, width, R),
                vmem(4, AL + 2, PL, R),
                vmem(4, AL, width, R),
                vmem(4, PL, R),
                vmem(2, 2, AL + 2, 1, R),
                vmem(2, AL, 1, R),
                vmem(2, 4, AL, 1, R),
                vmem(2, 16, R),
                vmem(2, 6, AL, 2, R),
                vmem(2, 6, AL, 2, R),
                vmem(2, 4, AL, 2, R),
                vmem(2, 4, AL, 2, R),
                vmem(4, 2, 1, R),
                vmem(4, 2, 1, R),
                dma(2), dma(14), dma(14), dma(6 * n_pitch), dma(6), dma(4),
            ],
            compiler_params=pltpu.CompilerParams(
                collective_id=0, has_side_effects=True, vmem_limit_bytes=56 * 2**20
            ),
        )(phase_angles, flow_state, node_offset, blade_mode, lag_series)

    placed = (
        P(None, "span", "pitch", None),
        P(None, "span", "pitch", None),
        P(None, "span", None),
        P(),
        P(None, None, None, None, "span", None),
    )
    return jax.shard_map(
        per_device,
        mesh=mesh,
        in_specs=placed,
        out_specs=(P(None, "span", "pitch", None), P(None, "span", "pitch", None)),
        check_vma=False,
    )
```

```python
import functools

import jax
import jax.numpy as jnp
from jax import lax
from jax.experimental import pallas as pl
from jax.experimental.pallas import tpu as pltpu
from jax.sharding import PartitionSpec as P

MESH = pl.DeviceIdType.MESH
F32 = jnp.float32
TIME_STEP = 0.25
DAMPING = 0.02
SECTION_WEIGHTS = (0.5, 1.0)
PAD = 8
CHUNK = 16


def kernel(
    n_pitch, n_span, AL, PL, R, HARM,
    phase, flow_hbm, node_hbm, mode, lag,
    state_out, moved_out,
    S0, S1, N, M, GE, H, G, RAD, W, MODE, CORR, TRIG, SB0, RB0, SB1, RB1, CS, CR,
    loc, send, recv, wsend, wrecv, osem,
):
    me_p = lax.axis_index("pitch")
    me_s = lax.axis_index("span")
    left = lax.rem(me_p + n_pitch - 1, n_pitch)
    right = lax.rem(me_p + 1, n_pitch)
    low_end = me_p == 0
    high_end = me_p == n_pitch - 1
    first = me_s == 0
    last = me_s == n_span - 1
    not_first = me_s > 0
    not_last = me_s < n_span - 1
    total_pitch = PL * n_pitch
    total_axial = AL * n_span
    lead = total_axial // 4
    lo, hi = PAD, PAD + PL
    def by_rows(count, body, step):
        def several(i, _):
            for j in range(step):
                body(i * step + j, 0)
            return 0

        lax.fori_loop(0, count // step, several, 0)

    def remote(src, dst, number, p, s):
        return pltpu.make_async_remote_copy(
            src_ref=src, dst_ref=dst, send_sem=send.at[number], recv_sem=recv.at[number],
            device_id=(p, s), device_id_type=MESH,
        )

    node_in = pltpu.make_async_copy(
        node_hbm, N.at[:, pl.ds(1, AL), pl.ds(lo, PL), :], loc.at[0]
    )
    flow_in = pltpu.make_async_copy(
        flow_hbm, S0.at[:, pl.ds(2, AL), pl.ds(lo, PL), :], loc.at[1]
    )
    node_in.start()
    flow_in.start()

    above = lax.rem(me_s + n_span - 1, n_span)
    below = lax.rem(me_s + 1, n_span)

    barrier = pltpu.get_barrier_semaphore()
    for step in range(1, n_pitch):
        other = lax.rem(me_p + step, n_pitch)
        pl.semaphore_signal(barrier, inc=1, device_id=(other, me_s), device_id_type=MESH)

    @pl.when(not_first)
    def _():
        for other in range(n_pitch):
            pl.semaphore_signal(
                barrier, inc=1, device_id=(other, above), device_id_type=MESH
            )

    @pl.when(not_last)
    def _():
        for other in range(n_pitch):
            pl.semaphore_signal(
                barrier, inc=1, device_id=(other, below), device_id_type=MESH
            )

    rows = lax.broadcasted_iota(jnp.int32, (16, R), 0)
    harmonic = jnp.where(rows < 2, 0, lax.rem(rows + 1, 3)) + 1
    move = jnp.where(rows == 1, 1, jnp.where(rows < 2, 0, jnp.where(rows < 5, -1, jnp.where(rows < 8, 0, 1))))
    now = phase[0]
    lagging = phase[1]
    angle = harmonic.astype(F32) * (now + move.astype(F32) * lagging)
    TRIG[0] = jnp.cos(angle)
    TRIG[1] = jnp.sin(angle)

    def trig(kind, row):
        return TRIG[kind, row:row + 1, :]

    for side, base in ((0, 2), (1, 8)):
        series = 1 - side
        for var in range(4):
            total = None
            for k in range(HARM):
                change_cos = trig(0, base + k) - trig(0, 5 + k)
                change_sin = trig(1, base + k) - trig(1, 5 + k)
                term = lag[series, k, 0, var] * change_cos - lag[series, k, 1, var] * change_sin
                total = term if total is None else total + term
            for a in range(AL):
                CORR[side, var, a] = total[a:a + 1, :]
    for part in range(2):
        for a in range(AL):
            MODE[part, a] = mode[part, a:a + 1, :]

    def blade_at(a):
        at = me_s * AL + a
        return (at >= lead) & (at < total_axial - lead)

    node_in.wait()

    def wall_rows(side, early, late):
        def body(a, _):
            nx = N[0, a + 1, late:late + 1, :] - N[0, a + 1, early:early + 1, :]
            ny = 1.0 + N[1, a + 1, late:late + 1, :] - N[1, a + 1, early:early + 1, :]
            length = jnp.sqrt(nx * nx + ny * ny)
            amp = MODE[0, a] * trig(0, side) - MODE[1, a] * trig(1, side)
            amp = jnp.where(blade_at(a), amp, 0.0)
            W[side, 0, a + 1] = amp * (nx / length)
            W[side, 1, a + 1] = amp * (ny / length)
            return 0

        by_rows(AL, body, 8)

    @pl.when(low_end)
    def _():
        wall_rows(0, lo, lo + 1)

    @pl.when(high_end)
    def _():
        wall_rows(1, hi - 2, hi - 1)

    for left_row, src in ((0, hi - 1), (1, lo)):
        for end, a in ((0, AL), (1, 1)):
            number = 2 * end + left_row
            CS[number] = N[:, a, src:src + 1, :]

    sides = jnp.where(not_first, 1, 0) + jnp.where(not_last, 1, 0)
    pl.semaphore_wait(barrier, n_pitch - 1 + n_pitch * sides)

    def wall_copy(side, kind, p, s, step):
        src, dst = ((1, 1), (1, AL + 1), (AL, 0))[kind]
        size = AL if kind == 0 else 1
        return pltpu.make_async_remote_copy(
            src_ref=W.at[side, :, pl.ds(src, size)],
            dst_ref=W.at[side, :, pl.ds(dst, size)],
            send_sem=wsend.at[(side * 3 + kind) * n_pitch + step],
            recv_sem=wrecv.at[side * 3 + kind],
            device_id=(p, s), device_id_type=MESH,
        )

    def walls(act):
        for side, own in ((0, low_end), (1, high_end)):
            @pl.when(own)
            def _(side=side):
                for step in range(1, n_pitch):
                    act(wall_copy(side, 0, lax.rem(me_p + step, n_pitch), me_s, step))

                @pl.when(not_first)
                def _():
                    for other in range(n_pitch):
                        act(wall_copy(side, 1, other, above, other))

                @pl.when(not_last)
                def _():
                    for other in range(n_pitch):
                        act(wall_copy(side, 2, other, below, other))

    walls(lambda copy: copy.start())

    field = pl.ds(lo, PL)
    node_up = remote(node_hbm.at[:, pl.ds(0, 1)], N.at[:, pl.ds(AL + 1, 1), field], 0, me_p, above)
    node_down = remote(node_hbm.at[:, pl.ds(AL - 1, 1)], N.at[:, pl.ds(0, 1), field], 1, me_p, below)
    flow_up = remote(flow_hbm.at[:, pl.ds(0, 2)], S0.at[:, pl.ds(AL + 2, 2), field], 2, me_p, above)
    flow_down = remote(flow_hbm.at[:, pl.ds(AL - 2, 2)], S0.at[:, pl.ds(0, 2), field], 3, me_p, below)
    to_left = remote(SB0.at[0], RB0.at[1], 4, left, me_s)
    to_right = remote(SB0.at[1], RB0.at[0], 5, right, me_s)
    corner_down = [
        remote(CS.at[0], CR.at[0], 6, right, below),
        remote(CS.at[1], CR.at[1], 7, left, below),
    ]
    corner_up = [
        remote(CS.at[2], CR.at[2], 8, right, above),
        remote(CS.at[3], CR.at[3], 9, left, above),
    ]
    next_up = remote(S1.at[:, pl.ds(2, 2), field], S1.at[:, pl.ds(AL + 2, 2), field], 10, me_p, above)
    next_down = remote(S1.at[:, pl.ds(AL, 2), field], S1.at[:, pl.ds(0, 2), field], 11, me_p, below)
    next_left = remote(SB1.at[0], RB1.at[1], 12, left, me_s)
    next_right = remote(SB1.at[1], RB1.at[0], 13, right, me_s)

    @pl.when(not_first)
    def _():
        node_up.start()
        for copy in corner_up:
            copy.start()
        flow_up.start()

    @pl.when(not_last)
    def _():
        node_down.start()
        for copy in corner_down:
            copy.start()
        flow_down.start()

    flow_in.wait()

    def pack(S, B):
        def body(a, _):
            for var in range(4):
                B[0, var, a] = S[var, a + 2, lo:lo + 2, :]
                B[1, var, a] = S[var, a + 2, hi - 2:hi, :]
            return 0

        by_rows(AL, body, 4)

    def pack_node(a, _):
        for var in range(2):
            SB0[0, 4 + var, a] = N[var, a + 1, lo:lo + 2, :]
            SB0[1, 4 + var, a] = N[var, a + 1, hi - 2:hi, :]
        return 0

    pack(S0, SB0)
    by_rows(AL, pack_node, 4)
    to_left.start()
    to_right.start()

    to_left.wait_recv()
    to_right.wait_recv()

    def node_edges(a, _):
        for var in range(2):
            N[var, a + 1, lo - 1:lo, :] = RB0[0, 4 + var, a, 1:2, :]
            N[var, a + 1, hi:hi + 1, :] = RB0[1, 4 + var, a, 0:1, :]
        return 0

    by_rows(AL, node_edges, 4)

    @pl.when(not_first)
    def _():
        node_down.wait_recv()
        for copy in corner_down:
            copy.wait_recv()
        N[:, 0, lo - 1:lo, :] = CR[0]
        N[:, 0, hi:hi + 1, :] = CR[1]

    @pl.when(not_last)
    def _():
        node_up.wait_recv()
        for copy in corner_up:
            copy.wait_recv()
        N[:, AL + 1, lo - 1:lo, :] = CR[2]
        N[:, AL + 1, hi:hi + 1, :] = CR[3]

    @pl.when(first)
    def _():
        for var in range(2):
            N[var, 0] = 2.0 * N[var, 1] - N[var, 2]

    @pl.when(last)
    def _():
        for var in range(2):
            N[var, AL + 1] = 2.0 * N[var, AL] - N[var, AL - 1]

    @pl.when(low_end)
    def _():
        def body(a, _):
            for var in range(2):
                N[var, a, lo - 1:lo, :] = 2.0 * N[var, a, lo:lo + 1, :] - N[var, a, lo + 1:lo + 2, :]
            return 0

        lax.fori_loop(0, AL + 2, body, 0)

    @pl.when(high_end)
    def _():
        def body(a, _):
            for var in range(2):
                N[var, a, hi:hi + 1, :] = 2.0 * N[var, a, hi - 1:hi, :] - N[var, a, hi - 2:hi - 1, :]
            return 0

        lax.fori_loop(0, AL + 2, body, 0)

    low_gate = jnp.where(low_end, 1.0, 0.0)
    high_gate = jnp.where(high_end, 1.0, 0.0)

    def pitch_edges(S, B):
        def body(a, _):
            blade = blade_at(a)
            low_wall = blade & low_end
            high_wall = blade & high_end
            for var in range(4):
                sign = -1.0 if var == 2 else 1.0
                low_corr = CORR[0, var, a] * low_gate
                high_corr = CORR[1, var, a] * high_gate
                for row in range(2):
                    mirror = S[var, a + 2, lo + 1 - row:lo + 2 - row, :] * sign
                    arrived = B[0, var, a, row:row + 1, :] + low_corr
                    S[var, a + 2, lo - 2 + row:lo - 1 + row, :] = jnp.where(low_wall, mirror, arrived)
                    mirror = S[var, a + 2, hi - 1 - row:hi - row, :] * sign
                    arrived = B[1, var, a, row:row + 1, :] + high_corr
                    S[var, a + 2, hi + row:hi + row + 1, :] = jnp.where(high_wall, mirror, arrived)
            return 0

        by_rows(AL, body, 4)

    inner = [(q, CHUNK) for q in range(lo, hi, CHUNK)]
    outer = [(0, PAD), (hi, PAD)]

    def along_pitch(T, a, q, size):
        return [
            T[comp, a, q + 1:q + 1 + size, :] - T[comp, a, q - 1:q - 1 + size, :] for comp in range(2)
        ]

    def along_axis(T, a, q, size):
        return [T[comp, a + 1, q:q + size, :] - T[comp, a - 1, q:q + size, :] for comp in range(2)]

    def old_row(i, _):
        a = i + 1
        for q, size in inner:
            px, py = along_pitch(N, a, q, size)
            zx, zy = along_axis(N, a, q, size)
            GE[6, a, q:q + size, :] = (2.0 + zx) * (2.0 + py) - px * zy
        return 0

    pitch_edges(S0, RB0)
    lax.fori_loop(0, AL, old_row, 0)

    for side, own in ((0, low_end), (1, high_end)):
        @pl.when(jnp.logical_not(own))
        def _(side=side):
            wall_copy(side, 0, me_p, me_s, 0).wait_recv()

        @pl.when(not_last)
        def _(side=side):
            wall_copy(side, 1, me_p, me_s, 0).wait_recv()

        @pl.when(not_first)
        def _(side=side):
            wall_copy(side, 2, me_p, me_s, 0).wait_recv()

        @pl.when(first)
        def _(side=side):
            W[side, :, 0] = 2.0 * W[side, :, 1] - W[side, :, 2]

        @pl.when(last)
        def _(side=side):
            W[side, :, AL + 1] = 2.0 * W[side, :, AL] - W[side, :, AL - 1]

    def shift_of(a, q, size):
        at = me_p * PL + (q - lo) + lax.broadcasted_iota(jnp.int32, (size, R), 0)
        blend = at.astype(F32) * (1.0 / (total_pitch - 1))
        out = []
        for comp in range(2):
            low = W[0, comp, a]
            out.append(low + blend * (W[1, comp, a] - low))
        return out

    def move_row(a, _):
        for q, size in outer + inner:
            for comp, shift in enumerate(shift_of(a, q, size)):
                M[comp, a, q:q + size, :] = N[comp, a, q:q + size, :] + shift
        return 0

    lax.fori_loop(0, AL + 2, move_row, 0)
    moved_copy = pltpu.make_async_copy(M.at[:, pl.ds(1, AL), field], moved_out, osem.at[0])
    moved_copy.start()

    def axial_terms(a, q, size):
        px, py = along_pitch(M, a, q, size)
        c, e = 2.0 + py, -px
        sx, sy = shift_of(a, q, size)
        GE[3, a, q:q + size, :] = c
        GE[4, a, q:q + size, :] = e
        GE[5, a, q:q + size, :] = (c * sx + e * sy) * (1.0 / TIME_STEP)
        return c, e

    def pitch_terms(a, q, size):
        zx, zy = along_axis(M, a, q, size)
        first_c, second_c = -zy, 2.0 + zx
        sx, sy = shift_of(a, q, size)
        GE[0, a, q:q + size, :] = first_c
        GE[1, a, q:q + size, :] = second_c
        GE[2, a, q:q + size, :] = (first_c * sx + second_c * sy) * (1.0 / TIME_STEP)
        return first_c, second_c

    def metric_row(i, _):
        a = i + 1
        for q, size in outer:
            pitch_terms(a, q, size)
        for q, size in inner:
            c, e = axial_terms(a, q, size)
            first_c, second_c = pitch_terms(a, q, size)
            new = second_c * c - e * first_c
            inverse = 1.0 / new
            GE[6, a, q:q + size, :] = GE[6, a, q:q + size, :] * inverse
            GE[7, a, q:q + size, :] = TIME_STEP * inverse
        return 0

    for a in (0, AL + 1):
        for q, size in inner:
            axial_terms(a, q, size)
    lax.fori_loop(0, AL, metric_row, 0)

    def flux(S, a, q, size, pitch, axial):
        r, mx, my, e = [S[var, a + 1, q:q + size, :] for var in range(4)]
        guess = pl.reciprocal(r, approx=True)
        inverse = guess * (2.0 - r * guess)
        u = mx * inverse
        v = my * inverse
        p = 0.4 * e - 0.2 * (mx * u + my * v)
        done = []
        for wanted, base in ((pitch, 0), (axial, 3)):
            if not wanted:
                done.append(None)
                continue
            c0, c1, sweep = [GE[base + j, a, q:q + size, :] for j in range(3)]
            w = c0 * u + c1 * v
            rel = w - sweep
            done.append((r * rel, mx * rel + c0 * p, my * rel + c1 * p, e * rel + p * w))
        return done

    def flux_field(S):
        def body(i, _):
            a = i + 1
            for q, size in inner:
                pitch_flux, axial_flux = flux(S, a, q, size, True, True)
                for var in range(4):
                    G[var, i, q:q + size, :] = pitch_flux[var]
                    H[var, a, q - lo:q - lo + size, :] = axial_flux[var]
            return 0

        lax.fori_loop(0, AL, body, 0)

    def flux_sides(S):
        def body(i, _):
            for q, size in outer:
                pitch_flux, _unused = flux(S, i + 1, q, size, True, False)
                for var in range(4):
                    G[var, i, q:q + size, :] = pitch_flux[var]
            return 0

        lax.fori_loop(0, AL, body, 0)

    def flux_ends(S):
        for a in (0, AL + 1):
            for q, size in inner:
                _unused, axial_flux = flux(S, a, q, size, False, True)
                for var in range(4):
                    H[var, a, q - lo:q - lo + size, :] = axial_flux[var]

    at_row = lax.broadcasted_iota(jnp.int32, (R, R), 0)
    at_col = lax.broadcasted_iota(jnp.int32, (R, R), 1)
    radial = jnp.zeros((R, R), F32)
    for offset, weight in ((-2, 1.0), (-1, -4.0), (0, 6.0), (1, -4.0), (2, 1.0)):
        source = jnp.clip(at_col + offset, 0, R - 1)
        radial = radial + jnp.where(at_row == source, weight, 0.0)
    radial = jnp.concatenate([radial, radial], axis=0).astype(jnp.bfloat16)

    def residual_row(S, i, weight, put):
        a = i + 2
        for var in range(4):
            values = S[var, a, lo:hi, :]
            head = values.astype(jnp.bfloat16)
            tail = (values - head.astype(F32)).astype(jnp.bfloat16)
            RAD[var] = jnp.dot(
                jnp.concatenate([head, tail], axis=1), radial, preferred_element_type=F32
            )
        for q, size in inner:
            keep = GE[6, i + 1, q:q + size, :]
            rate = GE[7, i + 1, q:q + size, :] * weight
            h = q - lo
            for var in range(4):
                here = S[var, a, q:q + size, :]
                near = (S[var, a, q + 1:q + 1 + size, :] + S[var, a, q - 1:q - 1 + size, :]) + (
                    S[var, a + 1, q:q + size, :] + S[var, a - 1, q:q + size, :]
                )
                far = (S[var, a, q + 2:q + 2 + size, :] + S[var, a, q - 2:q - 2 + size, :]) + (
                    S[var, a + 2, q:q + size, :] + S[var, a - 2, q:q + size, :]
                )
                fourth = (far + RAD[var, h:h + size, :]) + (12.0 * here - 4.0 * near)
                change = (G[var, i, q + 1:q + 1 + size, :] - G[var, i, q - 1:q - 1 + size, :]) + (
                    H[var, i + 2, h:h + size, :] - H[var, i, h:h + size, :]
                )
                value = keep * S0[var, a, q:q + size, :] - rate * (change + (4.0 * DAMPING) * fourth)
                put(var, i, q, size, value)

    def put_one(var, i, q, size, value):
        S1[var, i + 2, q:q + size, :] = value

    def put_two(var, i, q, size, value):
        S0[var, i + 2, q:q + size, :] = value

    def residual_inner(S, weight, put):
        def body(i, _):
            residual_row(S, i + 2, weight, put)
            return 0

        lax.fori_loop(0, AL - 4, body, 0)

    def residual_ends(S, weight, put):
        def body(i, _):
            residual_row(S, i + (AL - 4) * (i // 2), weight, put)
            return 0

        lax.fori_loop(0, 4, body, 0)

    def axial_edges(S, down, up):
        @pl.when(not_first)
        def _():
            down.wait_recv()

        @pl.when(not_last)
        def _():
            up.wait_recv()

        @pl.when(first)
        def _():
            for var in range(4):
                row = S[var, 2, lo:hi, :]
                S[var, 0, lo:hi, :] = row
                S[var, 1, lo:hi, :] = row

        @pl.when(last)
        def _():
            for var in range(4):
                row = S[var, AL + 1, lo:hi, :]
                S[var, AL + 2, lo:hi, :] = row
                S[var, AL + 3, lo:hi, :] = row

    flux_field(S0)
    flux_sides(S0)
    residual_inner(S0, SECTION_WEIGHTS[0], put_one)
    axial_edges(S0, flow_down, flow_up)
    flux_ends(S0)
    residual_ends(S0, SECTION_WEIGHTS[0], put_one)

    @pl.when(not_first)
    def _():
        next_up.start()

    @pl.when(not_last)
    def _():
        next_down.start()

    pack(S1, SB1)
    next_left.start()
    next_right.start()

    flux_field(S1)
    next_left.wait_recv()
    next_right.wait_recv()
    pitch_edges(S1, RB1)
    flux_sides(S1)
    residual_inner(S1, SECTION_WEIGHTS[1], put_two)
    out_inner = pltpu.make_async_copy(
        S0.at[:, pl.ds(4, AL - 4), field], state_out.at[:, pl.ds(2, AL - 4)], osem.at[1]
    )
    out_inner.start()
    axial_edges(S1, next_down, next_up)
    flux_ends(S1)
    residual_ends(S1, SECTION_WEIGHTS[1], put_two)
    out_first = pltpu.make_async_copy(
        S0.at[:, pl.ds(2, 2), field], state_out.at[:, pl.ds(0, 2)], osem.at[2]
    )
    out_last = pltpu.make_async_copy(
        S0.at[:, pl.ds(AL, 2), field], state_out.at[:, pl.ds(AL - 2, 2)], osem.at[3]
    )
    out_first.start()
    out_last.start()

    walls(lambda copy: copy.wait_send())

    @pl.when(not_first)
    def _():
        for copy in [node_up, flow_up, next_up] + corner_up:
            copy.wait_send()

    @pl.when(not_last)
    def _():
        for copy in [node_down, flow_down, next_down] + corner_down:
            copy.wait_send()

    for copy in (to_left, to_right, next_left, next_right):
        copy.wait_send()
    moved_copy.wait()
    out_inner.wait()
    out_first.wait()
    out_last.wait()


def solution(mesh):
    n_pitch = mesh.shape["pitch"]
    n_span = mesh.shape["span"]

    def per_device(flow_state, node_offset, blade_mode, phase_angles, lag_series):
        _, AL, PL, R = flow_state.shape
        HARM = lag_series.shape[1]
        width = PL + 2 * PAD
        vmem = lambda *shape: pltpu.VMEM(shape, F32)
        dma = lambda count: pltpu.SemaphoreType.DMA((count,))
        return pl.pallas_call(
            functools.partial(kernel, n_pitch, n_span, AL, PL, R, HARM),
            out_shape=(
                jax.ShapeDtypeStruct(flow_state.shape, F32),
                jax.ShapeDtypeStruct(node_offset.shape, F32),
            ),
            in_specs=[
                pl.BlockSpec(memory_space=pltpu.SMEM),
                pl.BlockSpec(memory_space=pl.ANY),
                pl.BlockSpec(memory_space=pl.ANY),
                pl.BlockSpec(memory_space=pltpu.VMEM),
                pl.BlockSpec(memory_space=pltpu.VMEM),
            ],
            out_specs=(pl.BlockSpec(memory_space=pl.ANY), pl.BlockSpec(memory_space=pl.ANY)),
            scratch_shapes=[
                vmem(4, AL + 4, width, R),
                vmem(4, AL + 4, width, R),
                vmem(2, AL + 2, width, R),
                vmem(2, AL + 2, width, R),
                vmem(8, AL + 2, width, R),
                vmem(4, AL + 2, PL, R),
                vmem(4, AL, width, R),
                vmem(4, PL, R),
                vmem(2, 2, AL + 2, 1, R),
                vmem(2, AL, 1, R),
                vmem(2, 4, AL, 1, R),
                vmem(2, 16, R),
                vmem(2, 6, AL, 2, R),
                vmem(2, 6, AL, 2, R),
                vmem(2, 4, AL, 2, R),
                vmem(2, 4, AL, 2, R),
                vmem(4, 2, 1, R),
                vmem(4, 2, 1, R),
                dma(2), dma(14), dma(14), dma(6 * n_pitch), dma(6), dma(4),
            ],
            compiler_params=pltpu.CompilerParams(
                collective_id=0, has_side_effects=True, vmem_limit_bytes=44 * 2**20
            ),
        )(phase_angles, flow_state, node_offset, blade_mode, lag_series)

    placed = (
        P(None, "span", "pitch", None),
        P(None, "span", "pitch", None),
        P(None, "span", None),
        P(),
        P(None, None, None, None, "span", None),
    )
    return jax.shard_map(
        per_device,
        mesh=mesh,
        in_specs=placed,
        out_specs=(P(None, "span", "pitch", None), P(None, "span", "pitch", None)),
        check_vma=False,
    )
```
